32 devices in a mesh: section: 4 (over y, x), tile: 8 (over z, core).
Axes of the slice: x: 2, y: 2, z: 4, core: 2. Of those that a mesh axis runs over, the one named last changes fastest.
Arguments:
- queries: bfloat16 [4, 4096, 2560], P('section', 'tile'), may hold values from -60 to 60
- keys_values: bfloat16 [4, 2, 4096, 2560], P('section', None, 'tile'), may hold values from -6 to 6
- windows: int32 [16, 2], P('tile'), may hold values from 0 to 1
- gate_scales: float32 [4, 2560], P('section'), may hold values from 0.5 to 3
- stream_in: bfloat16 [4096, 2560], P('tile'), may hold values from -3 to 3
Outputs:
- streams: bfloat16 [4, 4096, 2560], P('section', 'tile')
The draws below stay inside these ranges and needn't reach their ends.
All inputs are finite; a program needn't handle non-finite values.
Results may differ from the reference program's by a relative error of at most 0.005.
Values may be sent and summed in bfloat16 or wider, within the bound.
A program may use at most 128 MiB of HBM per device.

```python
import math
import jax
import jax.numpy as jnp
from jax import lax

HEAD_DIM = 128
HEADS = 20
TILE = 256
REACH = 1
BLOCKS = 4
TILES = 16
TOKENS = 4096


def shared_draw(key):
    base_key = jax.random.fold_in(key, 913)
    query_key, keys_key, values_key = jax.random.split(base_key, 3)
    width = HEADS * HEAD_DIM
    shape = (BLOCKS, TOKENS, width)
    queries = 1.4 * jnp.clip(jax.random.normal(query_key, shape, jnp.float32), -5.7, 5.7)
    keys = jnp.clip(jax.random.normal(keys_key, shape, jnp.float32), -6.0, 6.0)
    values = jnp.clip(jax.random.normal(values_key, shape, jnp.float32), -6.0, 6.0)
    return (queries, jnp.stack([keys, values], axis=1))


def draw_queries(key, part):
    return shared_draw(key)[0].astype(jnp.bfloat16)


def draw_keys_values(key, part):
    return shared_draw(key)[1].astype(jnp.bfloat16)


def with_ends(result, stream_key, low, largest):
    place = [jax.random.randint(jax.random.fold_in(stream_key, axis), (), 0, length) for axis, length in enumerate(result.shape)]
    longest = result.shape.index(max(result.shape))
    neighbour = place[:longest] + [(place[longest] + 1) % result.shape[longest]] + place[longest + 1:]
    return result.at[tuple(place)].set(low).at[tuple(neighbour)].set(largest)


def levels(rng, shape, pieces, smallest, largest):
    def one(axis_at, shards_of):
        draws = jax.random.uniform(jax.random.fold_in(jax.random.fold_in(rng, 6), axis_at), (shards_of,), jnp.float32, smallest / len(pieces), largest / len(pieces))
        return jnp.repeat(jnp.exp(draws), shape[axis_at] // shards_of).reshape((-1,) + (1,) * (len(shape) - axis_at - 1))

    gain = one(*pieces[0])
    for cut in pieces[1:]:
        gain = gain * one(*cut)
    return gain


def normal_values(stream_key, shape, deviation, reach, shards=(), held_as=jnp.bfloat16):
    array = jax.random.normal(stream_key, shape, jnp.float32) * deviation
    if len(shards) > 0:
        array = levels(stream_key, shape, shards, -0.22, 0.18) * array
    return jnp.clip(array, min=-reach, max=reach).astype(held_as)


def setup_inputs(seed: int = 0) -> dict:
    splits = jax.random.split(jax.random.key(seed), 6)
    queries = draw_queries(jax.random.fold_in(splits[5], 71), 0)
    keys_values = draw_keys_values(jax.random.fold_in(splits[5], 71), 0)
    windows = with_ends(jax.random.randint(splits[2], (TILES, 2), 0, REACH + 1), jax.random.fold_in(splits[2], 1), 0, REACH).astype(jnp.int32)
    gate_scales = jnp.clip(0.5 + 2.5 * jax.random.uniform(splits[3], (BLOCKS, HEADS * HEAD_DIM), jnp.float32) ** levels(splits[3], (BLOCKS, HEADS * HEAD_DIM), ((0, 4),), -0.2, 0.2), 0.5, 3.0)
    stream_in = normal_values(splits[4], (TOKENS, HEADS * HEAD_DIM), 0.5, 3.0, ((0, 8),))
    return {"queries": queries, "keys_values": keys_values, "windows": windows, "gate_scales": gate_scales, "stream_in": stream_in}


def reference(queries, keys_values, windows, gate_scales, stream_in):
    width = HEADS * HEAD_DIM
    border = jnp.zeros((BLOCKS, 2, REACH * TILE, width), jnp.bfloat16)
    padded = jnp.concatenate([border, keys_values, border], axis=2)
    key_span = (2 * REACH + 1) * TILE
    score_scale = 1.0 / math.sqrt(HEAD_DIM)

    def one_tile(tile_index):
        token_start = (tile_index * TILE).astype(jnp.int32)
        query_block = lax.dynamic_slice_in_dim(queries, token_start, TILE, 1).astype(jnp.float32)
        query_block = query_block.reshape(BLOCKS, TILE, HEADS, HEAD_DIM)
        pair_block = lax.dynamic_slice_in_dim(padded, token_start, key_span, 2).astype(jnp.float32)
        key_block = pair_block[:, 0].reshape(BLOCKS, key_span, HEADS, HEAD_DIM)
        value_block = pair_block[:, 1].reshape(BLOCKS, key_span, HEADS, HEAD_DIM)
        key_tile = tile_index - REACH + jnp.arange(key_span, dtype=jnp.int32) // TILE
        lower_reach = windows[tile_index, 0]
        upper_reach = windows[tile_index, 1]
        allowed = (key_tile >= tile_index - lower_reach) & (key_tile <= tile_index + upper_reach)
        allowed = allowed & (key_tile >= 0) & (key_tile < TILES)
        scores = jnp.einsum('bqhd,bkhd->bhqk', query_block, key_block, precision=lax.Precision.HIGHEST) * score_scale
        scores = jnp.where(allowed, scores, -jnp.inf)
        row_max = lax.optimization_barrier(jnp.max(scores, axis=-1, keepdims=True))
        exponent = jnp.exp(scores - row_max)
        weights = (exponent / lax.optimization_barrier(jnp.sum(exponent, axis=-1, keepdims=True))).astype(jnp.bfloat16)
        attended = jnp.einsum('bhqk,bkhd->bqhd', weights.astype(jnp.float32), value_block, precision=lax.Precision.HIGHEST)
        attended = attended.reshape(BLOCKS, TILE, width)
        return (gate_scales[:, None, :] * attended).astype(jnp.bfloat16)
    shares = lax.map(one_tile, jnp.arange(TILES, dtype=jnp.int32))
    shares = jnp.transpose(shares, (1, 0, 2, 3)).reshape(BLOCKS, TOKENS, width)
    running = stream_in.astype(jnp.float32)
    results = []
    for block_index in range(BLOCKS):
        running = running + shares[block_index].astype(jnp.float32)
        results.append(running.astype(jnp.bfloat16))
    return jnp.stack(results)
```

```python
import functools
import math

import jax
import jax.numpy as jnp
from jax import lax
from jax.experimental import pallas as pl
from jax.experimental.pallas import tpu as pltpu
from jax.sharding import PartitionSpec as P

HEAD_DIM = 128
TILE = 256
REACH = 1
HALO = REACH * TILE
LAG = 2
AHEAD = 3
FAR = 1e30
VMEM_BYTES = 56 * 1024 * 1024


def kernel(
    sections, tiles_axis,
    windows, queries, keys_values, gates, stream_in, out,
    q_buf, kv_buf, low, high, in_buf, share, recv, fwd, out_buf,
    q_sem, kv_sem, in_sem, out_sem, halo_send, halo_recv, sec_send, sec_recv,
):
    heads, rows = q_buf.shape[0], q_buf.shape[1]
    local_tiles = rows // TILE
    stages = sections.bit_length() - 1
    section = lax.axis_index("section")
    place = lax.axis_index("tile")
    has_left = place > 0
    has_right = place < tiles_axis - 1

    def partner(stage):
        d = 1 << stage
        return section + d - 2 * d * ((section // d) % 2)

    def sends(who, stage):
        return who // (1 << stage) < sections // (1 << stage) - 1

    def receives(stage):
        return sends(partner(stage), stage)

    def above(stage):
        return (section // (1 << stage)) % 2 == 1

    def columns(head):
        return pl.ds(pl.multiple_of(head * HEAD_DIM, HEAD_DIM), HEAD_DIM)

    def loads(head):
        cols = columns(head)
        return (
            pltpu.make_async_copy(
                keys_values.at[0, :, :, cols], kv_buf.at[head], kv_sem.at[head]
            ),
            pltpu.make_async_copy(queries.at[0, :, cols], q_buf.at[head], q_sem.at[head]),
            pltpu.make_async_copy(stream_in.at[:, cols], in_buf.at[head], in_sem.at[head]),
        )

    def to_right(head):
        return pltpu.make_async_remote_copy(
            src_ref=keys_values.at[0, :, pl.ds(rows - HALO, HALO), columns(head)],
            dst_ref=low.at[head],
            send_sem=halo_send.at[0, head],
            recv_sem=halo_recv.at[0, head],
            device_id={"tile": place + 1},
            device_id_type=pl.DeviceIdType.MESH,
        )

    def to_left(head):
        return pltpu.make_async_remote_copy(
            src_ref=keys_values.at[0, :, pl.ds(0, HALO), columns(head)],
            dst_ref=high.at[head],
            send_sem=halo_send.at[1, head],
            recv_sem=halo_recv.at[1, head],
            device_id={"tile": place - 1},
            device_id_type=pl.DeviceIdType.MESH,
        )

    def to_partner(stage, head):
        source = share.at[head] if stage == 0 else fwd.at[stage - 1, head]
        return pltpu.make_async_remote_copy(
            src_ref=source,
            dst_ref=recv.at[stage, head],
            send_sem=sec_send.at[stage, head],
            recv_sem=sec_recv.at[stage, head],
            device_id={"section": partner(stage)},
            device_id_type=pl.DeviceIdType.MESH,
        )

    def load(head):
        for copy in loads(head):
            copy.start()

    def send_halo(head):
        @pl.when(has_right)
        def _():
            to_right(head).start()

        @pl.when(has_left)
        def _():
            to_left(head).start()

    barrier = pltpu.get_barrier_semaphore()

    @pl.when(has_right)
    def _():
        pl.semaphore_signal(
            barrier, inc=1, device_id={"tile": place + 1}, device_id_type=pl.DeviceIdType.MESH
        )

    @pl.when(has_left)
    def _():
        pl.semaphore_signal(
            barrier, inc=1, device_id={"tile": place - 1}, device_id_type=pl.DeviceIdType.MESH
        )

    for stage in range(stages):
        pl.semaphore_signal(
            barrier, inc=1, device_id={"section": partner(stage)},
            device_id_type=pl.DeviceIdType.MESH,
        )
    ahead = min(AHEAD, heads)
    for head in range(ahead):
        load(head)

    def clear(ref):
        def one(head, carry):
            ref[head] = jnp.zeros(ref.shape[1:], ref.dtype)
            return carry

        lax.fori_loop(0, heads, one, 0)

    pl.when(jnp.logical_not(has_left))(lambda: clear(low))
    pl.when(jnp.logical_not(has_right))(lambda: clear(high))

    pl.semaphore_wait(barrier, stages + has_left.astype(jnp.int32) + has_right.astype(jnp.int32))
    for head in range(ahead):
        send_halo(head)

    factor = math.log2(math.e) / math.sqrt(HEAD_DIM)

    def attend(head):
        gate = gates[:, columns(head)]

        def block(index, which):
            if index < 0:
                return low[head, which, pl.ds((index + REACH) * TILE, TILE), :]
            if index >= local_tiles:
                return high[head, which, pl.ds((index - local_tiles) * TILE, TILE), :]
            return kv_buf[head, which, pl.ds(index * TILE, TILE), :]

        for tile in reversed(range(local_tiles)):
            span = pl.ds(tile * TILE, TILE)
            query = q_buf[head, span, :]
            offsets = range(-REACH, REACH + 1)
            at = place * local_tiles + tile
            allowed, scores, tops = [], [], []
            for offset in offsets:
                score = lax.dot_general(
                    query, block(tile + offset, 0), (((1,), (1,)), ((), ())),
                    preferred_element_type=jnp.float32,
                )
                top = jnp.max(score, axis=-1, keepdims=True)
                if offset < 0:
                    ok = (windows[tile, 0] >= -offset) & (at + offset >= 0)
                elif offset > 0:
                    ok = (windows[tile, 1] >= offset) & (at + offset < tiles_axis * local_tiles)
                else:
                    ok = None
                allowed.append(ok)
                scores.append(score)
                tops.append(top if ok is None else jnp.where(ok, top, -FAR))
            row_max = functools.reduce(jnp.maximum, tops)
            total = jnp.zeros((TILE, 1), jnp.float32)
            attended = jnp.zeros((TILE, HEAD_DIM), jnp.float32)
            for offset, ok, score in zip(offsets, allowed, scores):
                shift = row_max if ok is None else jnp.where(ok, row_max, FAR)
                weight = jnp.exp2((score - shift) * factor)
                total = total + jnp.sum(weight, axis=-1, keepdims=True)
                attended = attended + jnp.dot(
                    weight.astype(jnp.bfloat16), block(tile + offset, 1),
                    preferred_element_type=jnp.float32,
                )
            share[head, span, :] = (gate * (attended / total)).astype(jnp.bfloat16)

    def compute(head):
        @pl.when(head + ahead < heads)
        def _():
            load(head + ahead)
            send_halo(head + ahead)

        for copy in loads(head):
            copy.wait()

        @pl.when(has_right)
        def _():
            to_left(head).wait_recv()

        @pl.when(has_left)
        def _():
            to_right(head).wait_recv()

        attend(head)
        if stages > 0:
            @pl.when(sends(section, 0))
            def _():
                to_partner(0, head).start()

    def combine(stage, head):
        @pl.when(receives(stage))
        def _():
            to_partner(stage, head).wait_recv()

        if stage < stages - 1:
            @pl.when(sends(section, stage + 1))
            def _():
                held = share[head] if stage == 0 else fwd[stage - 1, head]
                both = held.astype(jnp.float32) + recv[stage, head].astype(jnp.float32)
                fwd[stage, head] = both.astype(jnp.bfloat16)
                to_partner(stage + 1, head).start()

    def finish(head):
        out_buf[head] = in_buf[head].astype(jnp.float32) + share[head].astype(jnp.float32)
        for stage in range(stages):
            @pl.when(above(stage))
            def _():
                out_buf[head] += recv[stage, head].astype(jnp.float32)
        in_buf[head] = out_buf[head].astype(jnp.bfloat16)
        result(head).start()

    def result(head):
        return pltpu.make_async_copy(
            in_buf.at[head], out.at[0, :, columns(head)], out_sem.at[head]
        )

    def step(count, carry):
        pl.when(count < heads)(lambda: compute(count))
        for stage in range(stages):
            head = count - (stage + 1) * LAG

            @pl.when((head >= 0) & (head < heads))
            def _():
                combine(stage, head)

        head = count - stages * LAG

        @pl.when((head >= 0) & (head < heads))
        def _():
            finish(head)

        return carry

    lax.fori_loop(0, heads + stages * LAG, step, 0)

    def drain(head, carry):
        result(head).wait()

        @pl.when(has_right)
        def _():
            to_right(head).wait_send()

        @pl.when(has_left)
        def _():
            to_left(head).wait_send()

        for stage in range(stages):
            @pl.when(sends(section, stage))
            def _():
                to_partner(stage, head).wait_send()

        return carry

    lax.fori_loop(0, heads, drain, 0)


def local(sections, tiles_axis, queries, keys_values, windows, gate_scales, stream_in):
    rows, width = queries.shape[1], queries.shape[2]
    heads = width // HEAD_DIM
    stages = sections.bit_length() - 1
    assert sections == 1 << stages
    half = (heads, rows, HEAD_DIM)
    anywhere = pl.BlockSpec(memory_space=pl.ANY)
    dma = pltpu.SemaphoreType.DMA
    return pl.pallas_call(
        functools.partial(kernel, sections, tiles_axis),
        out_shape=jax.ShapeDtypeStruct((1, rows, width), jnp.bfloat16),
        in_specs=[
            pl.BlockSpec(memory_space=pltpu.SMEM),
            anywhere,
            anywhere,
            pl.BlockSpec(memory_space=pltpu.VMEM),
            anywhere,
        ],
        out_specs=anywhere,
        scratch_shapes=[
            pltpu.VMEM(half, jnp.bfloat16),
            pltpu.VMEM((heads, 2, rows, HEAD_DIM), jnp.bfloat16),
            pltpu.VMEM((heads, 2, HALO, HEAD_DIM), jnp.bfloat16),
            pltpu.VMEM((heads, 2, HALO, HEAD_DIM), jnp.bfloat16),
            pltpu.VMEM(half, jnp.bfloat16),
            pltpu.VMEM(half, jnp.bfloat16),
            pltpu.VMEM((max(stages, 1),) + half, jnp.bfloat16),
            pltpu.VMEM((max(stages - 1, 1),) + half, jnp.bfloat16),
            pltpu.VMEM(half, jnp.float32),
            dma((heads,)),
            dma((heads,)),
            dma((heads,)),
            dma((heads,)),
            dma((2, heads)),
            dma((2, heads)),
            dma((max(stages, 1), heads)),
            dma((max(stages, 1), heads)),
        ],
        compiler_params=pltpu.CompilerParams(
            collective_id=0, has_side_effects=True, vmem_limit_bytes=VMEM_BYTES
        ),
    )(windows, queries, keys_values, gate_scales, stream_in)


def solution(mesh):
    placed = (
        P("section", "tile", None),
        P("section", None, "tile", None),
        P("tile", None),
        P("section", None),
        P("tile", None),
    )
    return jax.shard_map(
        functools.partial(local, mesh.shape["section"], mesh.shape["tile"]),
        mesh=mesh, in_specs=placed, out_specs=P("section", "tile", None), check_vma=False,
    )
```

```python
import functools
import math

import jax
import jax.numpy as jnp
from jax import lax
from jax.experimental import pallas as pl
from jax.experimental.pallas import tpu as pltpu
from jax.sharding import PartitionSpec as P

HEAD_DIM = 128
TILE = 256
REACH = 1
HALO = REACH * TILE
LAG = 3
AHEAD = 3
FAR = 1e30
VMEM_BYTES = 50 * 1024 * 1024


def kernel(
    sections, tiles_axis,
    windows, queries, keys_values, gates, stream_in, out,
    q_buf, kv_buf, low, high, in_buf, share, recv, fwd, out_buf,
    q_sem, kv_sem, in_sem, halo_send, halo_recv, sec_send, sec_recv,
):
    heads, rows = q_buf.shape[0], q_buf.shape[1]
    local_tiles = rows // TILE
    units = heads * local_tiles
    stages = sections.bit_length() - 1
    section = lax.axis_index("section")
    place = lax.axis_index("tile")
    has_left = place > 0
    has_right = place < tiles_axis - 1

    def partner(stage):
        d = 1 << stage
        return section + d - 2 * d * ((section // d) % 2)

    def sends(who, stage):
        return who // (1 << stage) < sections // (1 << stage) - 1

    def receives(stage):
        return sends(partner(stage), stage)

    def above(stage):
        return (section // (1 << stage)) % 2 == 1

    def columns(head):
        return pl.ds(pl.multiple_of(head * HEAD_DIM, HEAD_DIM), HEAD_DIM)

    def loads(head):
        cols = columns(head)
        return (
            pltpu.make_async_copy(
                keys_values.at[0, :, :, cols], kv_buf.at[head], kv_sem.at[head]
            ),
            pltpu.make_async_copy(queries.at[0, :, cols], q_buf.at[head], q_sem.at[head]),
            pltpu.make_async_copy(stream_in.at[:, cols], in_buf.at[head], in_sem.at[head]),
        )

    def to_right(head):
        return pltpu.make_async_remote_copy(
            src_ref=keys_values.at[0, :, pl.ds(rows - HALO, HALO), columns(head)],
            dst_ref=low.at[head],
            send_sem=halo_send.at[0, head],
            recv_sem=halo_recv.at[0, head],
            device_id={"tile": place + 1},
            device_id_type=pl.DeviceIdType.MESH,
        )

    def to_left(head):
        return pltpu.make_async_remote_copy(
            src_ref=keys_values.at[0, :, pl.ds(0, HALO), columns(head)],
            dst_ref=high.at[head],
            send_sem=halo_send.at[1, head],
            recv_sem=halo_recv.at[1, head],
            device_id={"tile": place - 1},
            device_id_type=pl.DeviceIdType.MESH,
        )

    def where(unit):
        head, order = unit // local_tiles, unit % local_tiles
        inner = place % 2
        tile = order * inner + (local_tiles - 1 - order) * (1 - inner)
        return head, tile, pl.ds(pl.multiple_of(tile * TILE, TILE), TILE)

    def to_partner(stage, unit):
        head, tile, span = where(unit)
        source = share.at[head, span] if stage == 0 else fwd.at[stage - 1, head, span]
        return pltpu.make_async_remote_copy(
            src_ref=source,
            dst_ref=recv.at[stage, head, span],
            send_sem=sec_send.at[stage, unit],
            recv_sem=sec_recv.at[stage, unit],
            device_id={"section": partner(stage)},
            device_id_type=pl.DeviceIdType.MESH,
        )

    def load(head):
        for copy in loads(head):
            copy.start()

    def send_halo(head):
        @pl.when(has_right)
        def _():
            to_right(head).start()

        @pl.when(has_left)
        def _():
            to_left(head).start()

    barrier = pltpu.get_barrier_semaphore()

    @pl.when(has_right)
    def _():
        pl.semaphore_signal(
            barrier, inc=1, device_id={"tile": place + 1}, device_id_type=pl.DeviceIdType.MESH
        )

    @pl.when(has_left)
    def _():
        pl.semaphore_signal(
            barrier, inc=1, device_id={"tile": place - 1}, device_id_type=pl.DeviceIdType.MESH
        )

    for stage in range(stages):
        pl.semaphore_signal(
            barrier, inc=1, device_id={"section": partner(stage)},
            device_id_type=pl.DeviceIdType.MESH,
        )
    ahead = min(AHEAD, heads)
    for head in range(ahead):
        load(head)

    def clear(ref):
        def one(head, carry):
            ref[head] = jnp.zeros(ref.shape[1:], ref.dtype)
            return carry

        lax.fori_loop(0, heads, one, 0)

    pl.when(jnp.logical_not(has_left))(lambda: clear(low))
    pl.when(jnp.logical_not(has_right))(lambda: clear(high))

    pl.semaphore_wait(barrier, stages + has_left.astype(jnp.int32) + has_right.astype(jnp.int32))
    for head in range(ahead):
        send_halo(head)

    factor = math.log2(math.e) / math.sqrt(HEAD_DIM)

    def attend(head, tile):
        gate = gates[:, columns(head)]

        def block(index, which):
            if index < 0:
                return low[head, which, pl.ds((index + REACH) * TILE, TILE), :]
            if index >= local_tiles:
                return high[head, which, pl.ds((index - local_tiles) * TILE, TILE), :]
            return kv_buf[head, which, pl.ds(index * TILE, TILE), :]

        span = pl.ds(tile * TILE, TILE)
        query = q_buf[head, span, :]
        offsets = range(-REACH, REACH + 1)
        at = place * local_tiles + tile
        allowed, scores, tops = [], [], []
        for offset in offsets:
            score = lax.dot_general(
                query, block(tile + offset, 0), (((1,), (1,)), ((), ())),
                preferred_element_type=jnp.float32,
            )
            top = jnp.max(score, axis=-1, keepdims=True)
            if offset < 0:
                ok = (windows[tile, 0] >= -offset) & (at + offset >= 0)
            elif offset > 0:
                ok = (windows[tile, 1] >= offset) & (at + offset < tiles_axis * local_tiles)
            else:
                ok = None
            allowed.append(ok)
            scores.append(score)
            tops.append(top if ok is None else jnp.where(ok, top, -FAR))
        row_max = functools.reduce(jnp.maximum, tops)
        total = jnp.zeros((TILE, 1), jnp.float32)
        attended = jnp.zeros((TILE, HEAD_DIM), jnp.float32)
        for offset, ok, score in zip(offsets, allowed, scores):
            shift = row_max if ok is None else jnp.where(ok, row_max, FAR)
            weight = jnp.exp2((score - shift) * factor)
            total = total + jnp.sum(weight, axis=-1, keepdims=True)
            attended = attended + jnp.dot(
                weight.astype(jnp.bfloat16), block(tile + offset, 1),
                preferred_element_type=jnp.float32,
            )
        share[head, span, :] = (gate * (attended / total)).astype(jnp.bfloat16)

    def compute(unit):
        head, tile, _ = where(unit)

        @pl.when(unit % local_tiles == 0)
        def _():
            @pl.when(head + ahead < heads)
            def _():
                load(head + ahead)
                send_halo(head + ahead)

            for copy in loads(head):
                copy.wait()

        for at in range(local_tiles):
            @pl.when(tile == at)
            def _():
                if at == 0:
                    @pl.when(has_left)
                    def _():
                        to_right(head).wait_recv()

                if at == local_tiles - 1:
                    @pl.when(has_right)
                    def _():
                        to_left(head).wait_recv()

                attend(head, at)

        if stages > 0:
            @pl.when(sends(section, 0))
            def _():
                to_partner(0, unit).start()

    def combine(stage, unit):
        @pl.when(receives(stage))
        def _():
            to_partner(stage, unit).wait_recv()

        if stage < stages - 1:
            @pl.when(sends(section, stage + 1))
            def _():
                head, tile, span = where(unit)
                held = share[head, span] if stage == 0 else fwd[stage - 1, head, span]
                both = held.astype(jnp.float32) + recv[stage, head, span].astype(jnp.float32)
                fwd[stage, head, span] = both.astype(jnp.bfloat16)
                to_partner(stage + 1, unit).start()

    def finish(unit):
        head, tile, span = where(unit)
        out_buf[...] = in_buf[head, span].astype(jnp.float32) + share[head, span].astype(jnp.float32)
        for stage in range(stages):
            @pl.when(above(stage))
            def _():
                out_buf[...] += recv[stage, head, span].astype(jnp.float32)
        out[0, span, columns(head)] = out_buf[...].astype(jnp.bfloat16)

    def step(count, carry):
        pl.when(count < units)(lambda: compute(count))
        for stage in range(stages):
            unit = count - (stage + 1) * LAG

            @pl.when((unit >= 0) & (unit < units))
            def _():
                combine(stage, unit)

        unit = count - stages * LAG

        @pl.when((unit >= 0) & (unit < units))
        def _():
            finish(unit)

        return carry

    lax.fori_loop(0, units + stages * LAG, step, 0)

    def drain(head, carry):
        @pl.when(has_right)
        def _():
            to_right(head).wait_send()

        @pl.when(has_left)
        def _():
            to_left(head).wait_send()

        return carry

    lax.fori_loop(0, heads, drain, 0)

    def drain_units(unit, carry):
        for stage in range(stages):
            @pl.when(sends(section, stage))
            def _():
                to_partner(stage, unit).wait_send()

        return carry

    lax.fori_loop(0, units, drain_units, 0)


def local(sections, tiles_axis, queries, keys_values, windows, gate_scales, stream_in):
    rows, width = queries.shape[1], queries.shape[2]
    heads = width // HEAD_DIM
    stages = sections.bit_length() - 1
    assert sections == 1 << stages
    half = (heads, rows, HEAD_DIM)
    units = heads * (rows // TILE)
    anywhere = pl.BlockSpec(memory_space=pl.ANY)
    dma = pltpu.SemaphoreType.DMA
    return pl.pallas_call(
        functools.partial(kernel, sections, tiles_axis),
        out_shape=jax.ShapeDtypeStruct((1, rows, width), jnp.bfloat16),
        in_specs=[
            pl.BlockSpec(memory_space=pltpu.SMEM),
            anywhere,
            anywhere,
            pl.BlockSpec(memory_space=pltpu.VMEM),
            anywhere,
        ],
        out_specs=pl.BlockSpec(memory_space=pltpu.VMEM),
        scratch_shapes=[
            pltpu.VMEM(half, jnp.bfloat16),
            pltpu.VMEM((heads, 2, rows, HEAD_DIM), jnp.bfloat16),
            pltpu.VMEM((heads, 2, HALO, HEAD_DIM), jnp.bfloat16),
            pltpu.VMEM((heads, 2, HALO, HEAD_DIM), jnp.bfloat16),
            pltpu.VMEM(half, jnp.bfloat16),
            pltpu.VMEM(half, jnp.bfloat16),
            pltpu.VMEM((max(stages, 1),) + half, jnp.bfloat16),
            pltpu.VMEM((max(stages - 1, 1),) + half, jnp.bfloat16),
            pltpu.VMEM((TILE, HEAD_DIM), jnp.float32),
            dma((heads,)),
            dma((heads,)),
            dma((heads,)),
            dma((2, heads)),
            dma((2, heads)),
            dma((max(stages, 1), units)),
            dma((max(stages, 1), units)),
        ],
        compiler_params=pltpu.CompilerParams(
            collective_id=0, has_side_effects=True, vmem_limit_bytes=VMEM_BYTES
        ),
    )(windows, queries, keys_values, gate_scales, stream_in)


def solution(mesh):
    placed = (
        P("section", "tile", None),
        P("section", None, "tile", None),
        P("tile", None),
        P("section", None),
        P("tile", None),
    )
    return jax.shard_map(
        functools.partial(local, mesh.shape["section"], mesh.shape["tile"]),
        mesh=mesh, in_specs=placed, out_specs=P("section", "tile", None), check_vma=False,
    )
```

```python
import functools
import math

import jax
import jax.numpy as jnp
from jax import lax
from jax.experimental import pallas as pl
from jax.experimental.pallas import tpu as pltpu
from jax.sharding import PartitionSpec as P

HEAD_DIM = 128
TILE = 256
REACH = 1
HALO = REACH * TILE
LAG = 3
AHEAD = 2
FAR = 1e30
VMEM_BYTES = 50 * 1024 * 1024


def kernel(
    sections, tiles_axis,
    windows_in, queries, keys_values, gates_in, stream_in, out,
    windows, gates, small_sem,
    q_buf, kv_buf, low, high, in_buf, share, recv, fwd, out_buf,
    q_sem, kv_sem, in_sem, halo_send, halo_recv, sec_send, sec_recv,
):
    heads, rows = q_buf.shape[0], q_buf.shape[1]
    local_tiles = rows // TILE
    units = heads * local_tiles
    stages = sections.bit_length() - 1
    section = lax.axis_index("section")
    place = lax.axis_index("tile")
    has_left = place > 0
    has_right = place < tiles_axis - 1

    def partner(stage):
        d = 1 << stage
        return section + d - 2 * d * ((section // d) % 2)

    def sends(who, stage):
        return who // (1 << stage) < sections // (1 << stage) - 1

    def receives(stage):
        return sends(partner(stage), stage)

    def above(stage):
        return (section // (1 << stage)) % 2 == 1

    def columns(head):
        return pl.ds(pl.multiple_of(head * HEAD_DIM, HEAD_DIM), HEAD_DIM)

    def loads(head):
        cols = columns(head)
        return (
            pltpu.make_async_copy(
                keys_values.at[0, :, :, cols], kv_buf.at[head], kv_sem.at[head]
            ),
            pltpu.make_async_copy(queries.at[0, :, cols], q_buf.at[head], q_sem.at[head]),
            pltpu.make_async_copy(stream_in.at[:, cols], in_buf.at[head], in_sem.at[head]),
        )

    def to_right(head):
        return pltpu.make_async_remote_copy(
            src_ref=keys_values.at[0, :, pl.ds(rows - HALO, HALO), columns(head)],
            dst_ref=low.at[head],
            send_sem=halo_send.at[0, head],
            recv_sem=halo_recv.at[0, head],
            device_id={"tile": place + 1},
            device_id_type=pl.DeviceIdType.MESH,
        )

    def to_left(head):
        return pltpu.make_async_remote_copy(
            src_ref=keys_values.at[0, :, pl.ds(0, HALO), columns(head)],
            dst_ref=high.at[head],
            send_sem=halo_send.at[1, head],
            recv_sem=halo_recv.at[1, head],
            device_id={"tile": place - 1},
            device_id_type=pl.DeviceIdType.MESH,
        )

    def where(unit):
        head, order = unit // local_tiles, unit % local_tiles
        inner = place % 2
        tile = order * inner + (local_tiles - 1 - order) * (1 - inner)
        return head, tile, pl.ds(pl.multiple_of(tile * TILE, TILE), TILE)

    def to_partner(stage, unit):
        head, tile, span = where(unit)
        source = share.at[head, span] if stage == 0 else fwd.at[stage - 1, head, span]
        return pltpu.make_async_remote_copy(
            src_ref=source,
            dst_ref=recv.at[stage, head, span],
            send_sem=sec_send.at[stage, unit],
            recv_sem=sec_recv.at[stage, unit],
            device_id={"section": partner(stage)},
            device_id_type=pl.DeviceIdType.MESH,
        )

    def load(head):
        for copy in loads(head):
            copy.start()

    def send_halo(head):
        @pl.when(has_right)
        def _():
            to_right(head).start()

        @pl.when(has_left)
        def _():
            to_left(head).start()

    small = (
        pltpu.make_async_copy(windows_in, windows, small_sem.at[0]),
        pltpu.make_async_copy(gates_in, gates, small_sem.at[1]),
    )
    barrier = pltpu.get_barrier_semaphore()

    @pl.when(has_right)
    def _():
        pl.semaphore_signal(
            barrier, inc=1, device_id={"tile": place + 1}, device_id_type=pl.DeviceIdType.MESH
        )

    @pl.when(has_left)
    def _():
        pl.semaphore_signal(
            barrier, inc=1, device_id={"tile": place - 1}, device_id_type=pl.DeviceIdType.MESH
        )

    for stage in range(stages):
        pl.semaphore_signal(
            barrier, inc=1, device_id={"section": partner(stage)},
            device_id_type=pl.DeviceIdType.MESH,
        )
    ahead = min(AHEAD, heads)
    for copy in small:
        copy.start()
    for head in range(ahead):
        load(head)

    pl.semaphore_wait(barrier, stages + has_left.astype(jnp.int32) + has_right.astype(jnp.int32))
    for head in range(ahead):
        send_halo(head)

    for copy in small:
        copy.wait()
    factor = math.log2(math.e) / math.sqrt(HEAD_DIM)

    def attend(head, tile):
        gate = gates[:, columns(head)]

        def block(index, which):
            if index < 0:
                return low[head, which, pl.ds((index + REACH) * TILE, TILE), :]
            if index >= local_tiles:
                return high[head, which, pl.ds((index - local_tiles) * TILE, TILE), :]
            return kv_buf[head, which, pl.ds(index * TILE, TILE), :]

        span = pl.ds(tile * TILE, TILE)
        query = q_buf[head, span, :]
        offsets = range(-REACH, REACH + 1)
        at = place * local_tiles + tile
        allowed, scores, tops = [], [], []
        for offset in offsets:
            score = lax.dot_general(
                query, block(tile + offset, 0), (((1,), (1,)), ((), ())),
                preferred_element_type=jnp.float32,
            )
            top = jnp.max(score, axis=-1, keepdims=True)
            if offset < 0:
                ok = (windows[tile, 0] >= -offset) & (at + offset >= 0)
            elif offset > 0:
                ok = (windows[tile, 1] >= offset) & (at + offset < tiles_axis * local_tiles)
            else:
                ok = None
            allowed.append(ok)
            scores.append(score)
            tops.append(top if ok is None else jnp.where(ok, top, -FAR))
        row_max = functools.reduce(jnp.maximum, tops)
        total = jnp.zeros((TILE, 1), jnp.float32)
        attended = jnp.zeros((TILE, HEAD_DIM), jnp.float32)
        for offset, ok, score in zip(offsets, allowed, scores):
            shift = row_max if ok is None else jnp.where(ok, row_max, FAR)
            weight = jnp.exp2((score - shift) * factor)
            total = total + jnp.sum(weight, axis=-1, keepdims=True)
            attended = attended + jnp.dot(
                weight.astype(jnp.bfloat16), block(tile + offset, 1),
                preferred_element_type=jnp.float32,
            )
        share[head, span, :] = (gate * (attended / total)).astype(jnp.bfloat16)

    def compute(unit):
        head, tile, _ = where(unit)

        @pl.when(unit % local_tiles == 0)
        def _():
            @pl.when(head + ahead < heads)
            def _():
                load(head + ahead)
                send_halo(head + ahead)

            for copy in loads(head):
                copy.wait()

            @pl.when(jnp.logical_not(has_left))
            def _():
                low[head] = jnp.zeros(low.shape[1:], low.dtype)

            @pl.when(jnp.logical_not(has_right))
            def _():
                high[head] = jnp.zeros(high.shape[1:], high.dtype)

        for at in range(local_tiles):
            @pl.when(tile == at)
            def _():
                if at == 0:
                    @pl.when(has_left)
                    def _():
                        to_right(head).wait_recv()

                if at == local_tiles - 1:
                    @pl.when(has_right)
                    def _():
                        to_left(head).wait_recv()

                attend(head, at)

        if stages > 0:
            @pl.when(sends(section, 0))
            def _():
                to_partner(0, unit).start()

    def combine(stage, unit):
        @pl.when(receives(stage))
        def _():
            to_partner(stage, unit).wait_recv()

        if stage < stages - 1:
            @pl.when(sends(section, stage + 1))
            def _():
                head, tile, span = where(unit)
                held = share[head, span] if stage == 0 else fwd[stage - 1, head, span]
                both = held.astype(jnp.float32) + recv[stage, head, span].astype(jnp.float32)
                fwd[stage, head, span] = both.astype(jnp.bfloat16)
                to_partner(stage + 1, unit).start()

    def finish(unit):
        head, tile, span = where(unit)
        out_buf[...] = in_buf[head, span].astype(jnp.float32) + share[head, span].astype(jnp.float32)
        for stage in range(stages):
            @pl.when(above(stage))
            def _():
                out_buf[...] += recv[stage, head, span].astype(jnp.float32)
        out[0, span, columns(head)] = out_buf[...].astype(jnp.bfloat16)

    def step(count, carry):
        pl.when(count < units)(lambda: compute(count))
        for stage in range(stages):
            unit = count - (stage + 1) * LAG

            @pl.when((unit >= 0) & (unit < units))
            def _():
                combine(stage, unit)

        unit = count - stages * LAG

        @pl.when((unit >= 0) & (unit < units))
        def _():
            finish(unit)

        return carry

    lax.fori_loop(0, units + stages * LAG, step, 0)

    def drain(head, carry):
        @pl.when(has_right)
        def _():
            to_right(head).wait_send()

        @pl.when(has_left)
        def _():
            to_left(head).wait_send()

        return carry

    lax.fori_loop(0, heads, drain, 0)

    def drain_units(unit, carry):
        for stage in range(stages):
            @pl.when(sends(section, stage))
            def _():
                to_partner(stage, unit).wait_send()

        return carry

    lax.fori_loop(0, units, drain_units, 0)


def local(sections, tiles_axis, queries, keys_values, windows, gate_scales, stream_in):
    rows, width = queries.shape[1], queries.shape[2]
    heads = width // HEAD_DIM
    stages = sections.bit_length() - 1
    assert sections == 1 << stages
    half = (heads, rows, HEAD_DIM)
    units = heads * (rows // TILE)
    anywhere = pl.BlockSpec(memory_space=pl.ANY)
    dma = pltpu.SemaphoreType.DMA
    return pl.pallas_call(
        functools.partial(kernel, sections, tiles_axis),
        out_shape=jax.ShapeDtypeStruct((1, rows, width), jnp.bfloat16),
        in_specs=[
            anywhere,
            anywhere,
            anywhere,
            anywhere,
            anywhere,
        ],
        out_specs=pl.BlockSpec(memory_space=pltpu.VMEM),
        scratch_shapes=[
            pltpu.SMEM(windows.shape, windows.dtype),
            pltpu.VMEM(gate_scales.shape, gate_scales.dtype),
            dma((2,)),
            pltpu.VMEM(half, jnp.bfloat16),
            pltpu.VMEM((heads, 2, rows, HEAD_DIM), jnp.bfloat16),
            pltpu.VMEM((heads, 2, HALO, HEAD_DIM), jnp.bfloat16),
            pltpu.VMEM((heads, 2, HALO, HEAD_DIM), jnp.bfloat16),
            pltpu.VMEM(half, jnp.bfloat16),
            pltpu.VMEM(half, jnp.bfloat16),
            pltpu.VMEM((max(stages, 1),) + half, jnp.bfloat16),
            pltpu.VMEM((max(stages - 1, 1),) + half, jnp.bfloat16),
            pltpu.VMEM((TILE, HEAD_DIM), jnp.float32),
            dma((heads,)),
            dma((heads,)),
            dma((heads,)),
            dma((2, heads)),
            dma((2, heads)),
            dma((max(stages, 1), units)),
            dma((max(stages, 1), units)),
        ],
        compiler_params=pltpu.CompilerParams(
            collective_id=0, has_side_effects=True, vmem_limit_bytes=VMEM_BYTES
        ),
    )(windows, queries, keys_values, gate_scales, stream_in)


def solution(mesh):
    placed = (
        P("section", "tile", None),
        P("section", None, "tile", None),
        P("tile", None),
        P("section", None),
        P("tile", None),
    )
    return jax.shard_map(
        functools.partial(local, mesh.shape["section"], mesh.shape["tile"]),
        mesh=mesh, in_specs=placed, out_specs=P("section", "tile", None), check_vma=False,
    )
```
